32 devices in a mesh: groups: 2 (over y), seq: 4 (over z), mp: 2 (over x), branch: 2 (over core).
Axes of the slice: x: 2, y: 2, z: 4, core: 2. Of those that a mesh axis runs over, the one named last changes fastest.
Arguments:
- streams: float32 [2, 8, 256, 1152], P('branch', ('groups', 'seq')), parts along dimension 1, may hold values from -6 to 6
- modulation: float32 [2, 6, 1152], P('branch'), may hold values from -3 to 3
- s_qkv: bfloat16 [2, 1152, 3, 1152], P('branch', 'seq', None, 'mp'), may hold values from -0.1875 to 0.1875
- s_out: bfloat16 [2, 1152, 1152], P('branch', 'mp', 'seq'), may hold values from -0.25 to 0.25
- w_in: bfloat16 [2, 1152, 4608], P('branch', 'seq', 'mp'), may hold values from -0.1875 to 0.1875
- w_out: bfloat16 [2, 4608, 1152], P('branch', 'mp', 'seq'), may hold values from -0.125 to 0.125
- hint_gain: float32 [13, 1152], replicated, may hold values from 0.3 to 3
- inject_layer: int32 [4], replicated, may hold values from 0 to 12
- hint_weight: bfloat16 [1152, 1152], P('seq', 'mp'), may hold values from -0.1875 to 0.1875
- t_mod: float32 [3, 1152], replicated, may hold values from -3 to 3
- t_qkv: bfloat16 [1152, 3, 1152], P('seq', None, 'mp'), may hold values from -0.1875 to 0.1875
- t_out: bfloat16 [1152, 1152], P('mp', 'seq'), may hold values from -0.25 to 0.25
Outputs:
- main_out: float32 [8, 256, 1152], P('groups', ('seq', 'branch'), 'mp'), parts along dimension 0
The draws below stay inside these ranges and needn't reach their ends.
There are 2 independent parts, one for each index of `groups`. The reference program is written for one: setup_inputs(seed, part) draws one part's arguments, and reference() takes and returns one part's arrays. A program takes and returns all parts, laid end to end along the dimension named above; an argument that names none is the same for every part. Nothing has to cross between parts.
All inputs are finite; a program needn't handle non-finite values.
Results may differ from the reference program's by a relative error of at most 0.014.
Values may be sent and summed in bfloat16 or wider, within the bound.
A program may use at most 64 MiB of HBM per device.

```python
import math
import jax
import jax.numpy as jnp
from jax import lax

D = 1152
FF = 4608
HEADS = 16
HEAD_DIM = 72
HINT_LAYERS = 13
TPF = 256
FRAMES = 4


def touch_ends(values, key, least, top_value):
    dims = values.shape
    index_at = [jax.random.randint(jax.random.fold_in(key, axis), (), 0, dims[axis]) for axis in range(len(dims))]
    values = values.at[tuple(index_at)].set(least)
    longest = dims.index(max(dims))
    index_at[longest] = (index_at[longest] + 1) % dims[longest]
    return values.at[tuple(index_at)].set(top_value)


def spiked(drawn, stream_key, source, target, shards_of, factor):
    def block_of(axis_at):
        return (jnp.arange(drawn.shape[axis_at]) // (drawn.shape[axis_at] // shards_of)).reshape((-1,) + (1,) * (drawn.ndim - 1 - axis_at))

    first = jax.random.permutation(stream_key, shards_of)[block_of(target)]
    second = (block_of(target) + shards_of // 2) % shards_of
    return jnp.where((block_of(source) == first) | (block_of(source) == second), factor * drawn, drawn)


def steps_of(stream_key, extent, pieces, low, high):
    level = 1.0
    for axis_at, parts in pieces:
        heights = jax.random.uniform(jax.random.fold_in(jax.random.fold_in(stream_key, 6), axis_at), (parts,), jnp.float32, low / len(pieces), high / len(pieces))
        level = level * jnp.repeat(jnp.exp(heights), extent[axis_at] // parts).reshape((-1,) + (1,) * (len(extent) - 1 - axis_at))
    return level


def bell_draw(rng, shape, spread, reach, pieces=(), kind=jnp.bfloat16):
    array = jax.random.normal(rng, shape, jnp.float32) * spread
    if len(pieces) > 0:
        array = steps_of(rng, shape, pieces, -0.22, 0.18) * array
    return jnp.clip(array, min=-reach, max=reach).astype(kind)


def bell_draw_with(key, shape, deviation, limit, split, heavy, held_as=jnp.bfloat16):
    values = deviation * jax.random.normal(key, shape, jnp.float32)
    if split:
        values = values * steps_of(key, shape, split, -0.22, 0.18)
    return jnp.clip(spiked(values, jax.random.fold_in(key, 3), *heavy), -limit, limit).astype(held_as)


def setup_inputs(seed: int = 0, part: int = 0) -> dict:
    splits = jax.random.split(jax.random.key(seed), 13)
    part_keys = jax.random.split(jax.random.fold_in(splits[12], part), 13)
    return {
        "streams": bell_draw(part_keys[0], (2, FRAMES, TPF, D), 1.0, 6.0, ((0, 2), (1, 4)), jnp.float32),
        "modulation": bell_draw(splits[1], (2, 6, D), 0.7, 3.0, ((0, 2),), jnp.float32),
        "s_qkv": bell_draw(splits[2], (2, D, 3, D), D ** -0.5, 0.1875, ((0, 2), (1, 4), (3, 2))),
        "s_out": bell_draw_with(splits[3], (2, D, D), D ** -0.5, 0.25, ((0, 2), (1, 2), (2, 4)), (1, 2, 4, 2.0)),
        "w_in": bell_draw(splits[4], (2, D, FF), D ** -0.5, 0.1875, ((0, 2), (1, 4), (2, 2))),
        "w_out": bell_draw_with(splits[5], (2, FF, D), FF ** -0.5, 0.125, ((0, 2), (1, 2), (2, 4)), (1, 2, 4, 2.0)),
        "hint_gain": jnp.clip(jnp.exp(jax.random.uniform(splits[6], (HINT_LAYERS, D), jnp.float32, math.log(0.3), math.log(3.0))), 0.3, 3.0),
        "inject_layer": touch_ends(jax.random.randint(splits[7], (FRAMES,), 0, HINT_LAYERS), jax.random.fold_in(splits[7], 1), 0, HINT_LAYERS - 1).astype(jnp.int32),
        "hint_weight": bell_draw(splits[8], (D, D), D ** -0.5, 0.1875, ((0, 4), (1, 2))),
        "t_mod": bell_draw(splits[9], (3, D), 0.7, 3.0, (), jnp.float32),
        "t_qkv": bell_draw(splits[10], (D, 3, D), D ** -0.5, 0.1875, ((0, 4), (2, 2))),
        "t_out": bell_draw_with(splits[11], (D, D), D ** -0.5, 0.25, ((0, 2), (1, 4)), (0, 1, 4, 2.0)),
    }


def layer_norm(value, shift, scale):
    mean = lax.optimization_barrier(jnp.mean(value, axis=-1, keepdims=True))
    centred = value - mean
    var = lax.optimization_barrier(jnp.mean(centred * centred, axis=-1, keepdims=True))
    return centred * lax.rsqrt(var + 1e-06) * (1.0 + scale) + shift

def attend(query, keys, values):
    scores = jnp.einsum('qhd,khd->hqk', query, keys, precision=lax.Precision.HIGHEST) / jnp.sqrt(jnp.float32(HEAD_DIM))
    weights = jnp.exp(scores)
    weights = weights / lax.optimization_barrier(jnp.sum(weights, axis=-1, keepdims=True))
    result = jnp.einsum('hqk,khd->qhd', weights, values, precision=lax.Precision.HIGHEST)
    return result.reshape(result.shape[0], -1)

def spatial_block(stream, mods, qkv_w, out_w, in_w, down_w):
    normed = layer_norm(stream, mods[0], mods[1]).astype(jnp.bfloat16)
    qkv = jnp.dot(normed, qkv_w.reshape(D, 3 * D), preferred_element_type=jnp.float32)
    qkv = qkv.reshape(TPF, 3, HEADS, HEAD_DIM)
    attended = attend(qkv[:, 0], qkv[:, 1], qkv[:, 2]).astype(jnp.bfloat16)
    stream = stream + mods[2] * jnp.dot(attended, out_w, preferred_element_type=jnp.float32)
    normed = layer_norm(stream, mods[3], mods[4]).astype(jnp.bfloat16)
    hidden = jax.nn.gelu(jnp.dot(normed, in_w, preferred_element_type=jnp.float32), approximate=True).astype(jnp.bfloat16)
    return stream + mods[5] * jnp.dot(hidden, down_w, preferred_element_type=jnp.float32)

def reference(streams, modulation, s_qkv, s_out, w_in, w_out, hint_gain, inject_layer, hint_weight, t_mod, t_qkv, t_out):
    outputs = []
    for section in range(2):

        def one_frame(frame, section=section):
            return spatial_block(frame, modulation[section], s_qkv[section], s_out[section], w_in[section], w_out[section])
        outputs.append(lax.map(one_frame, streams[section]))
    control, main = (outputs[0], outputs[1])
    picks = (inject_layer[:, None] == jnp.arange(HINT_LAYERS, dtype=jnp.int32)[None, :]).astype(jnp.float32)
    gain = lax.optimization_barrier(jnp.sum(picks[:, :, None] * hint_gain[None, :, :], axis=1))
    hint_in = (control * gain[:, None, :]).astype(jnp.bfloat16).reshape(FRAMES * TPF, D)
    joined = main.reshape(FRAMES * TPF, D) + jnp.dot(hint_in, hint_weight, preferred_element_type=jnp.float32)
    normed = layer_norm(joined, t_mod[0], t_mod[1]).astype(jnp.bfloat16)
    tqkv = jnp.dot(normed, t_qkv.reshape(D, 3 * D), preferred_element_type=jnp.float32)
    tqkv = tqkv.reshape(FRAMES, TPF, 3, HEADS, HEAD_DIM).transpose(1, 0, 2, 3, 4)
    attended = jax.vmap(attend)(tqkv[:, :, 0], tqkv[:, :, 1], tqkv[:, :, 2])
    attended = attended.transpose(1, 0, 2).reshape(FRAMES * TPF, D).astype(jnp.bfloat16)
    result = joined + t_mod[2] * jnp.dot(attended, t_out, preferred_element_type=jnp.float32)
    return result.reshape(FRAMES, TPF, D)
```

```python
import functools

import jax
import jax.numpy as jnp
from jax import lax
from jax.experimental import pallas as pl
from jax.experimental.pallas import tpu as pltpu
from jax.sharding import PartitionSpec as P

D = 1152
HEAD_DIM = 72
HINT_LAYERS = 13


def layer_norm(value, shift, scale):
    mean = jnp.mean(value, axis=-1, keepdims=True)
    centred = value - mean
    var = jnp.mean(centred * centred, axis=-1, keepdims=True)
    return centred * lax.rsqrt(var + 1e-06) * (1.0 + scale) + shift


def attend(query, keys, values):
    scores = jnp.einsum("qhd,khd->hqk", query, keys, precision=lax.Precision.HIGHEST) / jnp.sqrt(
        jnp.float32(HEAD_DIM)
    )
    weights = jnp.exp(scores)
    weights = weights / jnp.sum(weights, axis=-1, keepdims=True)
    result = jnp.einsum("hqk,khd->qhd", weights, values, precision=lax.Precision.HIGHEST)
    return result.reshape(result.shape[0], -1)


def row_product(left, piece):
    return jnp.dot(left, piece, preferred_element_type=jnp.float32)


def on_device(
    streams,
    modulation,
    s_qkv,
    s_out,
    w_in,
    w_out,
    hint_gain,
    inject_layer,
    hint_weight,
    t_mod,
    t_qkv,
    t_out,
):
    stream = streams[0, 0]
    mods = modulation[0]
    tokens = stream.shape[0]
    quarter = s_qkv.shape[3]
    offset = lax.axis_index("mp") * quarter
    local_heads = quarter // HEAD_DIM

    def share(vector):
        return lax.dynamic_slice_in_dim(vector, offset, quarter, 0)

    normed = layer_norm(stream, mods[0], mods[1]).astype(jnp.bfloat16)
    piece = lax.all_gather(s_qkv, "seq", axis=1, tiled=True)
    qkv = row_product(normed, piece[0].reshape(piece.shape[1], 3 * quarter))
    qkv = qkv.reshape(tokens, 3, local_heads, HEAD_DIM)
    attended = attend(qkv[:, 0], qkv[:, 1], qkv[:, 2]).astype(jnp.bfloat16)
    projected = jnp.dot(
        attended,
        lax.all_gather(s_out, "seq", axis=2, tiled=True)[0],
        preferred_element_type=jnp.float32,
    )
    partial_value = lax.psum_scatter(
        projected.astype(jnp.bfloat16), "mp", scatter_dimension=1, tiled=True
    ).astype(jnp.float32)
    stream_share = (
        lax.dynamic_slice_in_dim(stream, offset, quarter, 1) + share(mods[2]) * partial_value
    )
    stream = lax.all_gather(stream_share.astype(jnp.bfloat16), "mp", axis=1, tiled=True).astype(
        stream_share.dtype
    )
    normed = layer_norm(stream, mods[3], mods[4]).astype(jnp.bfloat16)
    upward = row_product(normed, lax.all_gather(w_in, "seq", axis=1, tiled=True)[0])
    hidden = jax.nn.gelu(upward, approximate=True).astype(jnp.bfloat16)
    downward = jnp.dot(
        hidden,
        lax.all_gather(w_out, "seq", axis=2, tiled=True)[0],
        preferred_element_type=jnp.float32,
    )
    mlp_part = lax.psum_scatter(
        downward.astype(jnp.bfloat16), "mp", scatter_dimension=1, tiled=True
    ).astype(jnp.float32)
    section_out = stream_share + share(mods[5]) * mlp_part
    moved = lax.all_to_all(
        lax.all_to_all(
            section_out[None, None].astype(jnp.bfloat16),
            "seq",
            split_axis=2,
            concat_axis=1,
            tiled=True,
        ),
        "branch",
        split_axis=2,
        concat_axis=0,
        tiled=True,
    ).astype(jnp.float32)
    frames = moved.shape[1]
    positions = moved.shape[2]
    rows = frames * positions
    control = moved[0]
    main_share = moved[1].reshape(rows, quarter)
    picks = (inject_layer[:, None] == jnp.arange(HINT_LAYERS, dtype=jnp.int32)[None, :]).astype(
        jnp.float32
    )
    gain = jnp.sum(picks[:, :, None] * hint_gain[None, :, :], axis=1)
    control_whole = lax.all_gather(control.astype(jnp.bfloat16), "mp", axis=2, tiled=True).astype(
        control.dtype
    )
    hint_in = (control_whole * gain[:, None, :]).astype(jnp.bfloat16).reshape(rows, D)
    hint = row_product(hint_in, lax.all_gather(hint_weight, "seq", axis=0, tiled=True))
    joined_share = main_share + hint
    joined = lax.all_gather(joined_share.astype(jnp.bfloat16), "mp", axis=1, tiled=True).astype(
        joined_share.dtype
    )
    normed_t = layer_norm(joined, t_mod[0], t_mod[1]).astype(jnp.bfloat16)
    piece = lax.all_gather(t_qkv, "seq", axis=0, tiled=True)
    tqkv = row_product(normed_t, piece.reshape(piece.shape[0], 3 * quarter))
    tqkv = tqkv.reshape(frames, positions, 3, local_heads, HEAD_DIM).transpose(1, 0, 2, 3, 4)
    attended_t = jax.vmap(attend)(tqkv[:, :, 0], tqkv[:, :, 1], tqkv[:, :, 2])
    attended_t = attended_t.transpose(1, 0, 2).reshape(rows, quarter).astype(jnp.bfloat16)
    projected_t = jnp.dot(
        attended_t,
        lax.all_gather(t_out, "seq", axis=1, tiled=True),
        preferred_element_type=jnp.float32,
    )
    temporal_part = lax.psum_scatter(
        projected_t.astype(jnp.bfloat16), "mp", scatter_dimension=1, tiled=True
    ).astype(jnp.float32)
    result = joined_share + share(t_mod[2]) * temporal_part
    return result.reshape(frames, positions, quarter)

F32, BF16 = jnp.float32, jnp.bfloat16


def dot(left, right):
    return jnp.dot(left, right, preferred_element_type=F32)


def dot_nt(left, right):
    return lax.dot_general(left, right, (((1,), (1,)), ((), ())), preferred_element_type=F32)


def fused_kernel(ring, *refs):
    n_weights = 7
    x_ref, mod_ref, gain_ref, tmod_ref = refs[:4]
    shards = refs[4 : 4 + n_weights]
    out_ref = refs[4 + n_weights]
    scratch = refs[5 + n_weights :]
    bufs = scratch[:n_weights]
    (qkv_ref, att_ref, x1_ref, send_ref, got_ref, got2_ref, hid_ref, yb_ref, moved_ref,
     js_ref, jr_ref, ts_ref, tr_ref, tq_ref, ta_ref, jf_ref) = scratch[n_weights : n_weights + 16]
    local_sem, right_sem, left_sem, z_sem, ysend_sem, y_sem, pair_send, pair_recv, move_send, move_recv = (
        scratch[n_weights + 16 :]
    )
    group, seq, mp, branch = (lax.axis_index(a) for a in ("groups", "seq", "mp", "branch"))
    depth = shards[0].shape[0]
    half = depth // 2
    other = 1 - group
    quarter = js_ref.shape[1]
    heads = quarter // HEAD_DIM

    def at(z=None, g=None, m=None, b=None):
        return (
            group if g is None else g,
            seq if z is None else z,
            mp if m is None else m,
            branch if b is None else b,
        )

    def remote(src, dst, send, recv, device):
        return pltpu.make_async_remote_copy(
            src_ref=src, dst_ref=dst, send_sem=send, recv_sem=recv,
            device_id=device, device_id_type=pl.DeviceIdType.MESH,
        )

    locals_ = []
    for w in range(n_weights):
        copy = pltpu.make_async_copy(
            shards[w], bufs[w].at[pl.ds(seq * depth, depth)], local_sem.at[w]
        )
        copy.start()
        locals_.append(copy)

    partners = [
        (lax.rem(seq + dz, ring), lax.rem(branch + db, 2))
        for dz in range(ring)
        for db in range(2)
        if dz or db
    ]
    barrier = pltpu.get_barrier_semaphore()
    greeted = [at(z=z, b=b) for z, b in partners] + [at(g=other), at(m=1 - mp)]
    for device in greeted:
        pl.semaphore_signal(barrier, inc=1, device_id=device, device_id_type=pl.DeviceIdType.MESH)
    pl.semaphore_wait(barrier, len(greeted))

    def block(w, s, g):
        return bufs[w].at[pl.ds(s * depth + g * half, half)]

    def rightward(w, s):
        ref = block(w, s, group)
        return remote(ref, ref, right_sem.at[w, s], z_sem.at[w, s], at(z=lax.rem(seq + 1, ring)))

    def leftward(w, s):
        ref = block(w, s, group)
        return remote(ref, ref, left_sem.at[w, s], z_sem.at[w, s], at(z=lax.rem(seq + ring - 1, ring)))

    def across(w, s, g):
        ref = block(w, s, g)
        return remote(ref, ref, ysend_sem.at[w, s], y_sem.at[w, s], at(g=other))

    def own(w):
        locals_[w].wait()

        @pl.when(seq < ring - 1)
        def _():
            rightward(w, seq).start()

        @pl.when(seq > 0)
        def _():
            leftward(w, seq).start()

    def step(w, d):
        @pl.when(seq - d >= 0)
        def _():
            s = seq - d
            rightward(w, s).wait_recv()

            @pl.when(seq < ring - 1)
            def _():
                rightward(w, s).start()

            across(w, s, group).start()

        @pl.when(seq + d < ring)
        def _():
            s = seq + d
            leftward(w, s).wait_recv()

            @pl.when(seq > 0)
            def _():
                leftward(w, s).start()

            across(w, s, group).start()

    def finish(w):
        for d in range(1, ring):

            @pl.when(seq - d >= 0)
            def _():
                across(w, seq - d, other).wait_recv()

            @pl.when(seq + d < ring)
            def _():
                across(w, seq + d, other).wait_recv()

    def drain(w):
        @pl.when(seq < ring - 1)
        def _():
            rightward(w, seq).wait_send()

        @pl.when(seq > 0)
        def _():
            leftward(w, seq).wait_send()

        for d in range(1, ring):

            @pl.when(seq - d >= 0)
            def _():
                across(w, seq - d, group).wait_send()

                @pl.when(seq < ring - 1)
                def _():
                    rightward(w, seq - d).wait_send()

            @pl.when(seq + d < ring)
            def _():
                across(w, seq + d, group).wait_send()

                @pl.when(seq > 0)
                def _():
                    leftward(w, seq + d).wait_send()

    def pair(i, src, dst):
        return remote(src, dst, pair_send.at[i], pair_recv.at[i], at(m=1 - mp))

    scale = 1.0 / (HEAD_DIM**0.5)
    own(0)
    own(1)
    normed = layer_norm(x_ref[...], mod_ref[0:1], mod_ref[1:2]).astype(BF16)
    step(0, 1)
    own(2)
    for d in range(2, ring):
        step(0, d)
    step(1, 1)
    own(3)
    for d in range(2, ring):
        step(1, d)
    finish(0)
    qkv_ref[...] = dot(normed, bufs[0][...])
    for i in range(heads):
        lo = i * HEAD_DIM
        query = (qkv_ref[:, lo : lo + HEAD_DIM] * scale).astype(BF16)
        keys = qkv_ref[:, quarter + lo : quarter + lo + HEAD_DIM].astype(BF16)
        values = qkv_ref[:, 2 * quarter + lo : 2 * quarter + lo + HEAD_DIM].astype(BF16)
        weights = jnp.exp(dot_nt(query, keys))
        total = jnp.sum(weights, axis=-1, keepdims=True)
        att_ref[:, lo : lo + HEAD_DIM] = dot(weights.astype(BF16), values) / total
    finish(1)
    projected = dot_nt(att_ref[...].astype(BF16), bufs[1][...])
    send_ref[0] = projected.astype(BF16)
    pair0 = pair(0, send_ref.at[0], got_ref)
    pair0.start()
    x1_ref[...] = x_ref[...] + mod_ref[2:3] * projected
    step(2, 1)
    own(4)
    step(2, 2) if ring > 2 else None
    pair0.wait_recv()
    x1_ref[...] += mod_ref[2:3] * got_ref[...].astype(F32)
    normed = layer_norm(x1_ref[...], mod_ref[3:4], mod_ref[4:5]).astype(BF16)
    for d in range(3, ring):
        step(2, d)
    step(3, 1)
    own(5)
    finish(2)
    send_ref[1] = normed
    wide = bufs[2].shape[1]
    tile = 768 if wide % 768 == 0 else wide

    def up(c, _):
        cols = pl.ds(pl.multiple_of(c * tile, tile), tile)
        hid_ref[:, cols] = jax.nn.gelu(dot(send_ref[1], bufs[2][:, cols]), approximate=True).astype(BF16)
        return 0

    lax.fori_loop(0, wide // tile, up, 0)
    for d in range(2, ring):
        step(3, d)
    own(6)
    step(4, 1)
    finish(3)
    down = dot_nt(hid_ref[...], bufs[3][...])
    send_ref[2] = down.astype(BF16)
    pair1 = pair(1, send_ref.at[2], got2_ref)
    pair1.start()
    x1_ref[...] += mod_ref[5:6] * down
    for d in range(2, ring):
        step(4, d)
    step(5, 1)
    pair1.wait_recv()
    yb_ref[...] = (x1_ref[...] + mod_ref[5:6] * got2_ref[...].astype(F32)).astype(BF16)
    positions = moved_ref.shape[2]

    def rows_of(z, b):
        return pl.ds(pl.multiple_of((z * 2 + b) * positions, positions), positions)

    sends = []
    for i, (z, b) in enumerate(partners):
        copy = remote(
            yb_ref.at[rows_of(z, b)], moved_ref.at[branch, seq],
            move_send.at[i], move_recv.at[branch, seq], at(z=z, b=b),
        )
        copy.start()
        sends.append(copy)
    moved_ref[branch, seq] = yb_ref[rows_of(seq, branch), :]
    for d in range(2, ring):
        step(5, d)
    step(6, 1)
    for z, b in partners:
        remote(
            yb_ref.at[rows_of(seq, branch)], moved_ref.at[b, z],
            move_send.at[0], move_recv.at[b, z], at(z=z, b=b),
        ).wait_recv()
    finish(4)
    rows = ring * positions
    hint_in = (moved_ref[0].astype(F32) * gain_ref[...][:, None, :]).astype(BF16)
    hint = dot(hint_in.reshape(rows, D), bufs[4][...])
    main = moved_ref[1].astype(F32).reshape(rows, D)
    first = mp == 0

    def share(value):
        return jnp.where(first, value[:, :quarter], value[:, quarter:])

    joined_share = share(main) + hint
    js_ref[...] = joined_share.astype(BF16)
    pair2 = pair(2, js_ref, jr_ref)
    pair2.start()
    for d in range(2, ring):
        step(6, d)
    finish(5)
    pair2.wait_recv()
    mine, theirs = joined_share, jr_ref[...].astype(F32)
    jf_ref[:, :quarter] = jnp.where(first, mine, theirs)
    jf_ref[:, quarter:] = jnp.where(first, theirs, mine)
    normed = layer_norm(jf_ref[...], tmod_ref[0:1], tmod_ref[1:2]).astype(BF16)
    tq_ref[...] = dot(normed, bufs[5][...])
    place = lax.rem(lax.broadcasted_iota(jnp.int32, (rows, rows), 0), positions)
    place_k = lax.rem(lax.broadcasted_iota(jnp.int32, (rows, rows), 1), positions)
    same = place == place_k
    for i in range(heads):
        lo = i * HEAD_DIM
        query = (tq_ref[:, lo : lo + HEAD_DIM] * scale).astype(BF16)
        keys = tq_ref[:, quarter + lo : quarter + lo + HEAD_DIM].astype(BF16)
        values = tq_ref[:, 2 * quarter + lo : 2 * quarter + lo + HEAD_DIM].astype(BF16)
        weights = jnp.where(same, jnp.exp(dot_nt(query, keys)), 0.0)
        total = jnp.sum(weights, axis=-1, keepdims=True)
        ta_ref[:, lo : lo + HEAD_DIM] = dot(weights.astype(BF16), values) / total
    finish(6)
    projected = dot_nt(ta_ref[...].astype(BF16), bufs[6][...])
    ts_ref[...] = jnp.where(first, projected[:, quarter:], projected[:, :quarter]).astype(BF16)
    pair3 = pair(3, ts_ref, tr_ref)
    pair3.start()
    for w in range(n_weights):
        drain(w)
    for copy in sends:
        copy.wait_send()
    pair3.wait_recv()
    gate = share(tmod_ref[2:3])
    out_ref[...] = joined_share + gate * (share(projected) + tr_ref[...].astype(F32))
    for copy in (pair0, pair1, pair2, pair3):
        copy.wait_send()


def fused(
    streams, modulation, s_qkv, s_out, w_in, w_out, hint_gain, inject_layer, hint_weight, t_mod, t_qkv, t_out
):
    ring = inject_layer.shape[0]
    tokens, quarter = streams.shape[2], s_qkv.shape[3]
    positions = tokens // (2 * ring)
    rows = ring * positions
    gain = hint_gain[inject_layer]
    depth = s_qkv.shape[1]
    shards = [
        s_qkv[0].reshape(depth, 3 * quarter),
        s_out[0].T,
        w_in[0],
        w_out[0].T,
        hint_weight,
        t_qkv.reshape(depth, 3 * quarter),
        t_out.T,
    ]
    n = len(shards)
    dma = pltpu.SemaphoreType.DMA
    vmem = pl.BlockSpec(memory_space=pltpu.VMEM)
    anywhere = pl.BlockSpec(memory_space=pl.ANY)
    out = pl.pallas_call(
        functools.partial(fused_kernel, ring),
        out_shape=jax.ShapeDtypeStruct((rows, quarter), F32),
        in_specs=[vmem] * 4 + [anywhere] * n,
        out_specs=vmem,
        scratch_shapes=[pltpu.VMEM((ring * depth, a.shape[1]), BF16) for a in shards]
        + [
            pltpu.VMEM((tokens, 3 * quarter), F32),
            pltpu.VMEM((tokens, quarter), F32),
            pltpu.VMEM((tokens, D), F32),
            pltpu.VMEM((3, tokens, D), BF16),
            pltpu.VMEM((tokens, D), BF16),
            pltpu.VMEM((tokens, D), BF16),
            pltpu.VMEM((tokens, w_in.shape[2]), BF16),
            pltpu.VMEM((tokens, D), BF16),
            pltpu.VMEM((2, ring, positions, D), BF16),
            pltpu.VMEM((rows, quarter), BF16),
            pltpu.VMEM((rows, quarter), BF16),
            pltpu.VMEM((rows, quarter), BF16),
            pltpu.VMEM((rows, quarter), BF16),
            pltpu.VMEM((rows, 3 * quarter), F32),
            pltpu.VMEM((rows, quarter), F32),
            pltpu.VMEM((rows, D), F32),
            dma((n,)),
            dma((n, ring)),
            dma((n, ring)),
            dma((n, ring)),
            dma((n, ring)),
            dma((n, ring)),
            dma((4,)),
            dma((4,)),
            dma((2 * ring - 1,)),
            dma((2, ring)),
        ],
        compiler_params=pltpu.CompilerParams(
            collective_id=0, has_side_effects=True, vmem_limit_bytes=50 * 1024 * 1024
        ),
    )(streams[0, 0], modulation[0], gain, t_mod, *shards)
    return out.reshape(ring, positions, quarter)


def solution(mesh):
    sizes = dict(mesh.shape)
    fits = (sizes["groups"], sizes["mp"], sizes["branch"]) == (2, 2, 2) and sizes["seq"] in (2, 4)
    in_specs = (
        P("branch", ("groups", "seq"), None, None),
        P("branch", None, None),
        P("branch", "seq", None, "mp"),
        P("branch", "mp", "seq"),
        P("branch", "seq", "mp"),
        P("branch", "mp", "seq"),
        P(),
        P(),
        P("seq", "mp"),
        P(),
        P("seq", None, "mp"),
        P("mp", "seq"),
    )
    out_specs = P("groups", ("seq", "branch"), "mp")
    return jax.shard_map(
        fused if fits else on_device, mesh=mesh, in_specs=in_specs, out_specs=out_specs, check_vma=False
    )
```

```python
import functools

import jax
import jax.numpy as jnp
from jax import lax
from jax.experimental import pallas as pl
from jax.experimental.pallas import tpu as pltpu
from jax.sharding import PartitionSpec as P

D = 1152
HEAD_DIM = 72
HINT_LAYERS = 13


def layer_norm(value, shift, scale):
    mean = jnp.mean(value, axis=-1, keepdims=True)
    centred = value - mean
    var = jnp.mean(centred * centred, axis=-1, keepdims=True)
    return centred * lax.rsqrt(var + 1e-06) * (1.0 + scale) + shift


def attend(query, keys, values):
    scores = jnp.einsum("qhd,khd->hqk", query, keys, precision=lax.Precision.HIGHEST) / jnp.sqrt(
        jnp.float32(HEAD_DIM)
    )
    weights = jnp.exp(scores)
    weights = weights / jnp.sum(weights, axis=-1, keepdims=True)
    result = jnp.einsum("hqk,khd->qhd", weights, values, precision=lax.Precision.HIGHEST)
    return result.reshape(result.shape[0], -1)


def row_product(left, piece):
    return jnp.dot(left, piece, preferred_element_type=jnp.float32)


def on_device(
    streams,
    modulation,
    s_qkv,
    s_out,
    w_in,
    w_out,
    hint_gain,
    inject_layer,
    hint_weight,
    t_mod,
    t_qkv,
    t_out,
):
    stream = streams[0, 0]
    mods = modulation[0]
    tokens = stream.shape[0]
    quarter = s_qkv.shape[3]
    offset = lax.axis_index("mp") * quarter
    local_heads = quarter // HEAD_DIM

    def share(vector):
        return lax.dynamic_slice_in_dim(vector, offset, quarter, 0)

    normed = layer_norm(stream, mods[0], mods[1]).astype(jnp.bfloat16)
    piece = lax.all_gather(s_qkv, "seq", axis=1, tiled=True)
    qkv = row_product(normed, piece[0].reshape(piece.shape[1], 3 * quarter))
    qkv = qkv.reshape(tokens, 3, local_heads, HEAD_DIM)
    attended = attend(qkv[:, 0], qkv[:, 1], qkv[:, 2]).astype(jnp.bfloat16)
    projected = jnp.dot(
        attended,
        lax.all_gather(s_out, "seq", axis=2, tiled=True)[0],
        preferred_element_type=jnp.float32,
    )
    partial_value = lax.psum_scatter(
        projected.astype(jnp.bfloat16), "mp", scatter_dimension=1, tiled=True
    ).astype(jnp.float32)
    stream_share = (
        lax.dynamic_slice_in_dim(stream, offset, quarter, 1) + share(mods[2]) * partial_value
    )
    stream = lax.all_gather(stream_share.astype(jnp.bfloat16), "mp", axis=1, tiled=True).astype(
        stream_share.dtype
    )
    normed = layer_norm(stream, mods[3], mods[4]).astype(jnp.bfloat16)
    upward = row_product(normed, lax.all_gather(w_in, "seq", axis=1, tiled=True)[0])
    hidden = jax.nn.gelu(upward, approximate=True).astype(jnp.bfloat16)
    downward = jnp.dot(
        hidden,
        lax.all_gather(w_out, "seq", axis=2, tiled=True)[0],
        preferred_element_type=jnp.float32,
    )
    mlp_part = lax.psum_scatter(
        downward.astype(jnp.bfloat16), "mp", scatter_dimension=1, tiled=True
    ).astype(jnp.float32)
    section_out = stream_share + share(mods[5]) * mlp_part
    moved = lax.all_to_all(
        lax.all_to_all(
            section_out[None, None].astype(jnp.bfloat16),
            "seq",
            split_axis=2,
            concat_axis=1,
            tiled=True,
        ),
        "branch",
        split_axis=2,
        concat_axis=0,
        tiled=True,
    ).astype(jnp.float32)
    frames = moved.shape[1]
    positions = moved.shape[2]
    rows = frames * positions
    control = moved[0]
    main_share = moved[1].reshape(rows, quarter)
    picks = (inject_layer[:, None] == jnp.arange(HINT_LAYERS, dtype=jnp.int32)[None, :]).astype(
        jnp.float32
    )
    gain = jnp.sum(picks[:, :, None] * hint_gain[None, :, :], axis=1)
    control_whole = lax.all_gather(control.astype(jnp.bfloat16), "mp", axis=2, tiled=True).astype(
        control.dtype
    )
    hint_in = (control_whole * gain[:, None, :]).astype(jnp.bfloat16).reshape(rows, D)
    hint = row_product(hint_in, lax.all_gather(hint_weight, "seq", axis=0, tiled=True))
    joined_share = main_share + hint
    joined = lax.all_gather(joined_share.astype(jnp.bfloat16), "mp", axis=1, tiled=True).astype(
        joined_share.dtype
    )
    normed_t = layer_norm(joined, t_mod[0], t_mod[1]).astype(jnp.bfloat16)
    piece = lax.all_gather(t_qkv, "seq", axis=0, tiled=True)
    tqkv = row_product(normed_t, piece.reshape(piece.shape[0], 3 * quarter))
    tqkv = tqkv.reshape(frames, positions, 3, local_heads, HEAD_DIM).transpose(1, 0, 2, 3, 4)
    attended_t = jax.vmap(attend)(tqkv[:, :, 0], tqkv[:, :, 1], tqkv[:, :, 2])
    attended_t = attended_t.transpose(1, 0, 2).reshape(rows, quarter).astype(jnp.bfloat16)
    projected_t = jnp.dot(
        attended_t,
        lax.all_gather(t_out, "seq", axis=1, tiled=True),
        preferred_element_type=jnp.float32,
    )
    temporal_part = lax.psum_scatter(
        projected_t.astype(jnp.bfloat16), "mp", scatter_dimension=1, tiled=True
    ).astype(jnp.float32)
    result = joined_share + share(t_mod[2]) * temporal_part
    return result.reshape(frames, positions, quarter)

F32, BF16 = jnp.float32, jnp.bfloat16


def dot(left, right):
    return jnp.dot(left, right, preferred_element_type=F32)


def dot_nt(left, right):
    return lax.dot_general(left, right, (((1,), (1,)), ((), ())), preferred_element_type=F32)


def fused_kernel(ring, *refs):
    n_weights = 6
    x_ref, mod_ref, gain_ref, tmod_ref = refs[:4]
    shards = refs[4 : 4 + n_weights]
    out_ref = refs[4 + n_weights]
    scratch = refs[5 + n_weights :]
    bufs = scratch[:n_weights]
    (qkv_ref, att_ref, x1_ref, send_ref, got_ref, got2_ref, hid_ref, yb_ref, moved_ref,
     js_ref, jr_ref, ts_ref, tr_ref, tq_ref, ta_ref, jf_ref) = scratch[n_weights : n_weights + 16]
    local_sem, right_sem, left_sem, z_sem, ysend_sem, y_sem, pair_send, pair_recv, move_send, move_recv, core_send, core_recv = (
        scratch[n_weights + 16 :]
    )
    group, seq, mp, branch = (lax.axis_index(a) for a in ("groups", "seq", "mp", "branch"))
    depth = shards[0].shape[0]
    half = depth // 2
    other = 1 - group
    quarter = js_ref.shape[1]
    heads = quarter // HEAD_DIM

    def at(z=None, g=None, m=None, b=None):
        return (
            group if g is None else g,
            seq if z is None else z,
            mp if m is None else m,
            branch if b is None else b,
        )

    def remote(src, dst, send, recv, device):
        return pltpu.make_async_remote_copy(
            src_ref=src, dst_ref=dst, send_sem=send, recv_sem=recv,
            device_id=device, device_id_type=pl.DeviceIdType.MESH,
        )

    shared = 4
    locals_ = []
    for w in range(n_weights):
        copy = pltpu.make_async_copy(
            shards[w],
            bufs[w].at[:, pl.ds(seq * depth, depth)] if w == shared else bufs[w].at[pl.ds(seq * depth, depth)],
            local_sem.at[w],
        )
        copy.start()
        locals_.append(copy)

    partners = [
        (lax.rem(seq + dz, ring), lax.rem(branch + db, 2))
        for dz in range(ring)
        for db in range(2)
        if dz or db
    ]
    barrier = pltpu.get_barrier_semaphore()
    greeted = [at(z=z, b=b) for z, b in partners] + [at(g=other), at(m=1 - mp)]
    for device in greeted:
        pl.semaphore_signal(barrier, inc=1, device_id=device, device_id_type=pl.DeviceIdType.MESH)
    pl.semaphore_wait(barrier, len(greeted))

    def block(w, s, g):
        rows = pl.ds(s * depth + g * half, half)
        return bufs[w].at[branch, rows] if w == shared else bufs[w].at[rows]

    def over(kind, s):
        ref = block(shared, s, other if kind else group)
        return remote(ref, ref, core_send.at[kind, s], core_recv.at[kind, s], at(b=1 - branch))

    def over_wait(kind, s):
        g = other if kind else group
        ref = bufs[shared].at[1 - branch, pl.ds(s * depth + g * half, half)]
        remote(ref, ref, core_send.at[kind, s], core_recv.at[kind, s], at(b=1 - branch)).wait_recv()

    def rightward(w, s):
        ref = block(w, s, group)
        return remote(ref, ref, right_sem.at[w, s], z_sem.at[w, s], at(z=lax.rem(seq + 1, ring)))

    def leftward(w, s):
        ref = block(w, s, group)
        return remote(ref, ref, left_sem.at[w, s], z_sem.at[w, s], at(z=lax.rem(seq + ring - 1, ring)))

    def across(w, s, g):
        ref = block(w, s, g)
        return remote(ref, ref, ysend_sem.at[w, s], y_sem.at[w, s], at(g=other))

    def own(w):
        locals_[w].wait()

        @pl.when(seq < ring - 1)
        def _():
            rightward(w, seq).start()

        @pl.when(seq > 0)
        def _():
            leftward(w, seq).start()

    def step(w, d):
        @pl.when(seq - d >= 0)
        def _():
            s = seq - d
            rightward(w, s).wait_recv()

            @pl.when(seq < ring - 1)
            def _():
                rightward(w, s).start()

            across(w, s, group).start()
            if w == shared:
                over(0, s).start()

        @pl.when(seq + d < ring)
        def _():
            s = seq + d
            leftward(w, s).wait_recv()

            @pl.when(seq > 0)
            def _():
                leftward(w, s).start()

            across(w, s, group).start()
            if w == shared:
                over(0, s).start()

    def finish(w):
        for d in range(1, ring):

            for sign in (-1, 1):
                s = seq + sign * d

                @pl.when((s >= 0) & (s < ring))
                def _():
                    across(w, s, other).wait_recv()
                    if w == shared:
                        over(1, s).start()

    def finish_shared():
        for d in range(1, ring):
            for sign in (-1, 1):
                s = seq + sign * d

                @pl.when((s >= 0) & (s < ring))
                def _():
                    over_wait(0, s)
                    over_wait(1, s)

    def drain(w):
        @pl.when(seq < ring - 1)
        def _():
            rightward(w, seq).wait_send()

        @pl.when(seq > 0)
        def _():
            leftward(w, seq).wait_send()

        for d in range(1, ring):

            @pl.when(seq - d >= 0)
            def _():
                across(w, seq - d, group).wait_send()
                if w == shared:
                    over(0, seq - d).wait_send()
                    over(1, seq - d).wait_send()

                @pl.when(seq < ring - 1)
                def _():
                    rightward(w, seq - d).wait_send()

            @pl.when(seq + d < ring)
            def _():
                across(w, seq + d, group).wait_send()
                if w == shared:
                    over(0, seq + d).wait_send()
                    over(1, seq + d).wait_send()

                @pl.when(seq > 0)
                def _():
                    leftward(w, seq + d).wait_send()

    def pair(i, src, dst):
        return remote(src, dst, pair_send.at[i], pair_recv.at[i], at(m=1 - mp))

    scale = 1.0 / (HEAD_DIM**0.5)
    own(0)
    own(1)
    normed = layer_norm(x_ref[...], mod_ref[0:1], mod_ref[1:2]).astype(BF16)
    step(0, 1)
    own(2)
    for d in range(2, ring):
        step(0, d)
    step(1, 1)
    own(3)
    for d in range(2, ring):
        step(1, d)
    finish(0)
    qkv_ref[...] = dot(normed, bufs[0][...])
    for i in range(heads):
        lo = i * HEAD_DIM
        query = (qkv_ref[:, lo : lo + HEAD_DIM] * scale).astype(BF16)
        keys = qkv_ref[:, quarter + lo : quarter + lo + HEAD_DIM].astype(BF16)
        values = qkv_ref[:, 2 * quarter + lo : 2 * quarter + lo + HEAD_DIM].astype(BF16)
        weights = jnp.exp(dot_nt(query, keys))
        total = jnp.sum(weights, axis=-1, keepdims=True)
        att_ref[:, lo : lo + HEAD_DIM] = dot(weights.astype(BF16), values) / total
        if i == heads // 2:
            step(2, 1)
            own(4)
    finish(1)
    projected = dot_nt(att_ref[...].astype(BF16), bufs[1][...])
    send_ref[0] = projected.astype(BF16)
    pair0 = pair(0, send_ref.at[0], got_ref)
    pair0.start()
    x1_ref[...] = x_ref[...] + mod_ref[2:3] * projected
    step(2, 2) if ring > 2 else None
    pair0.wait_recv()
    x1_ref[...] += mod_ref[2:3] * got_ref[...].astype(F32)
    normed = layer_norm(x1_ref[...], mod_ref[3:4], mod_ref[4:5]).astype(BF16)
    for d in range(3, ring):
        step(2, d)
    step(3, 1)
    own(5)
    finish(2)
    send_ref[1] = normed
    wide = bufs[2].shape[1]
    tile = 768 if wide % 768 == 0 else wide

    def up(c, _):
        cols = pl.ds(pl.multiple_of(c * tile, tile), tile)
        hid_ref[:, cols] = jax.nn.gelu(dot(send_ref[1], bufs[2][:, cols]), approximate=True).astype(BF16)
        return 0

    lax.fori_loop(0, wide // tile, up, 0)
    for d in range(2, ring):
        step(3, d)
    step(4, 1)
    finish(3)
    down = dot_nt(hid_ref[...], bufs[3][...])
    send_ref[2] = down.astype(BF16)
    pair1 = pair(1, send_ref.at[2], got2_ref)
    pair1.start()
    x1_ref[...] += mod_ref[5:6] * down
    for d in range(2, ring):
        step(4, d)
    step(5, 1)
    pair1.wait_recv()
    yb_ref[...] = (x1_ref[...] + mod_ref[5:6] * got2_ref[...].astype(F32)).astype(BF16)
    positions = moved_ref.shape[2]

    def rows_of(z, b):
        return pl.ds(pl.multiple_of((z * 2 + b) * positions, positions), positions)

    sends = []
    for i, (z, b) in enumerate(partners):
        copy = remote(
            yb_ref.at[rows_of(z, b)], moved_ref.at[branch, seq],
            move_send.at[i], move_recv.at[branch, seq], at(z=z, b=b),
        )
        copy.start()
        sends.append(copy)
    moved_ref[branch, seq] = yb_ref[rows_of(seq, branch), :]
    for d in range(2, ring):
        step(5, d)
    finish(4)
    for z, b in partners:
        remote(
            yb_ref.at[rows_of(seq, branch)], moved_ref.at[b, z],
            move_send.at[0], move_recv.at[b, z], at(z=z, b=b),
        ).wait_recv()
    finish_shared()
    rows = ring * positions
    hint_in = (moved_ref[0].astype(F32) * gain_ref[...][:, None, :]).astype(BF16)
    hint = dot(hint_in.reshape(rows, D), bufs[4][1, :, quarter:])
    main = moved_ref[1].astype(F32).reshape(rows, D)
    first = mp == 0

    def share(value):
        return jnp.where(first, value[:, :quarter], value[:, quarter:])

    joined_share = share(main) + hint
    js_ref[...] = joined_share.astype(BF16)
    pair2 = pair(2, js_ref, jr_ref)
    pair2.start()
    pair2.wait_recv()
    mine, theirs = joined_share, jr_ref[...].astype(F32)
    jf_ref[:, :quarter] = jnp.where(first, mine, theirs)
    jf_ref[:, quarter:] = jnp.where(first, theirs, mine)
    normed = layer_norm(jf_ref[...], tmod_ref[0:1], tmod_ref[1:2]).astype(BF16)
    tq_ref[:, : 2 * quarter] = dot(normed, bufs[4][0])
    tq_ref[:, 2 * quarter :] = dot(normed, bufs[4][1, :, :quarter])
    place = lax.rem(lax.broadcasted_iota(jnp.int32, (rows, rows), 0), positions)
    place_k = lax.rem(lax.broadcasted_iota(jnp.int32, (rows, rows), 1), positions)
    same = place == place_k
    for i in range(heads):
        lo = i * HEAD_DIM
        query = (tq_ref[:, lo : lo + HEAD_DIM] * scale).astype(BF16)
        keys = tq_ref[:, quarter + lo : quarter + lo + HEAD_DIM].astype(BF16)
        values = tq_ref[:, 2 * quarter + lo : 2 * quarter + lo + HEAD_DIM].astype(BF16)
        weights = jnp.where(same, jnp.exp(dot_nt(query, keys)), 0.0)
        total = jnp.sum(weights, axis=-1, keepdims=True)
        ta_ref[:, lo : lo + HEAD_DIM] = dot(weights.astype(BF16), values) / total
    finish(5)
    projected = dot_nt(ta_ref[...].astype(BF16), bufs[5][...])
    ts_ref[...] = jnp.where(first, projected[:, quarter:], projected[:, :quarter]).astype(BF16)
    pair3 = pair(3, ts_ref, tr_ref)
    pair3.start()
    for w in range(n_weights):
        drain(w)
    for copy in sends:
        copy.wait_send()
    pair3.wait_recv()
    gate = share(tmod_ref[2:3])
    out_ref[...] = joined_share + gate * (share(projected) + tr_ref[...].astype(F32))
    for copy in (pair0, pair1, pair2, pair3):
        copy.wait_send()


def fused(
    streams, modulation, s_qkv, s_out, w_in, w_out, hint_gain, inject_layer, hint_weight, t_mod, t_qkv, t_out
):
    ring = inject_layer.shape[0]
    tokens, quarter = streams.shape[2], s_qkv.shape[3]
    positions = tokens // (2 * ring)
    rows = ring * positions
    gain = hint_gain[inject_layer]
    depth = s_qkv.shape[1]
    shards = [
        s_qkv[0].reshape(depth, 3 * quarter),
        s_out[0].T,
        w_in[0],
        w_out[0].T,
        jnp.concatenate([t_qkv.reshape(depth, 3 * quarter), hint_weight], axis=1)
        .reshape(depth, 2, 2 * quarter)
        .transpose(1, 0, 2),
        t_out.T,
    ]
    n = len(shards)
    dma = pltpu.SemaphoreType.DMA
    vmem = pl.BlockSpec(memory_space=pltpu.VMEM)
    anywhere = pl.BlockSpec(memory_space=pl.ANY)
    out = pl.pallas_call(
        functools.partial(fused_kernel, ring),
        out_shape=jax.ShapeDtypeStruct((rows, quarter), F32),
        in_specs=[vmem] * 4 + [anywhere] * n,
        out_specs=vmem,
        scratch_shapes=[pltpu.VMEM(a.shape[:-2] + (ring * depth, a.shape[-1]), BF16) for a in shards]
        + [
            pltpu.VMEM((tokens, 3 * quarter), F32),
            pltpu.VMEM((tokens, quarter), F32),
            pltpu.VMEM((tokens, D), F32),
            pltpu.VMEM((3, tokens, D), BF16),
            pltpu.VMEM((tokens, D), BF16),
            pltpu.VMEM((tokens, D), BF16),
            pltpu.VMEM((tokens, w_in.shape[2]), BF16),
            pltpu.VMEM((tokens, D), BF16),
            pltpu.VMEM((2, ring, positions, D), BF16),
            pltpu.VMEM((rows, quarter), BF16),
            pltpu.VMEM((rows, quarter), BF16),
            pltpu.VMEM((rows, quarter), BF16),
            pltpu.VMEM((rows, quarter), BF16),
            pltpu.VMEM((rows, 3 * quarter), F32),
            pltpu.VMEM((rows, quarter), F32),
            pltpu.VMEM((rows, D), F32),
            dma((n,)),
            dma((n, ring)),
            dma((n, ring)),
            dma((n, ring)),
            dma((n, ring)),
            dma((n, ring)),
            dma((4,)),
            dma((4,)),
            dma((2 * ring - 1,)),
            dma((2, ring)),
            dma((2, ring)),
            dma((2, ring)),
        ],
        compiler_params=pltpu.CompilerParams(
            collective_id=0, has_side_effects=True, vmem_limit_bytes=50 * 1024 * 1024
        ),
    )(streams[0, 0], modulation[0], gain, t_mod, *shards)
    return out.reshape(ring, positions, quarter)


def solution(mesh):
    sizes = dict(mesh.shape)
    fits = (sizes["groups"], sizes["mp"], sizes["branch"]) == (2, 2, 2) and sizes["seq"] in (2, 4)
    in_specs = (
        P("branch", ("groups", "seq"), None, None),
        P("branch", None, None),
        P("branch", "seq", None, "mp"),
        P("branch", "mp", "seq"),
        P("branch", "seq", "mp"),
        P("branch", "mp", "seq"),
        P(),
        P(),
        P("seq", "mp"),
        P(),
        P("seq", None, "mp"),
        P("mp", "seq"),
    )
    out_specs = P("groups", ("seq", "branch"), "mp")
    return jax.shard_map(
        fused if fits else on_device, mesh=mesh, in_specs=in_specs, out_specs=out_specs, check_vma=False
    )
```

```python
import functools

import jax
import jax.numpy as jnp
from jax import lax
from jax.experimental import pallas as pl
from jax.experimental.pallas import tpu as pltpu
from jax.sharding import PartitionSpec as P

D = 1152
HEAD_DIM = 72
HINT_LAYERS = 13


def layer_norm(value, shift, scale):
    mean = jnp.mean(value, axis=-1, keepdims=True)
    centred = value - mean
    var = jnp.mean(centred * centred, axis=-1, keepdims=True)
    return centred * lax.rsqrt(var + 1e-06) * (1.0 + scale) + shift


def attend(query, keys, values):
    scores = jnp.einsum("qhd,khd->hqk", query, keys, precision=lax.Precision.HIGHEST) / jnp.sqrt(
        jnp.float32(HEAD_DIM)
    )
    weights = jnp.exp(scores)
    weights = weights / jnp.sum(weights, axis=-1, keepdims=True)
    result = jnp.einsum("hqk,khd->qhd", weights, values, precision=lax.Precision.HIGHEST)
    return result.reshape(result.shape[0], -1)


def row_product(left, piece):
    return jnp.dot(left, piece, preferred_element_type=jnp.float32)


def on_device(
    streams,
    modulation,
    s_qkv,
    s_out,
    w_in,
    w_out,
    hint_gain,
    inject_layer,
    hint_weight,
    t_mod,
    t_qkv,
    t_out,
):
    stream = streams[0, 0]
    mods = modulation[0]
    tokens = stream.shape[0]
    quarter = s_qkv.shape[3]
    offset = lax.axis_index("mp") * quarter
    local_heads = quarter // HEAD_DIM

    def share(vector):
        return lax.dynamic_slice_in_dim(vector, offset, quarter, 0)

    normed = layer_norm(stream, mods[0], mods[1]).astype(jnp.bfloat16)
    piece = lax.all_gather(s_qkv, "seq", axis=1, tiled=True)
    qkv = row_product(normed, piece[0].reshape(piece.shape[1], 3 * quarter))
    qkv = qkv.reshape(tokens, 3, local_heads, HEAD_DIM)
    attended = attend(qkv[:, 0], qkv[:, 1], qkv[:, 2]).astype(jnp.bfloat16)
    projected = jnp.dot(
        attended,
        lax.all_gather(s_out, "seq", axis=2, tiled=True)[0],
        preferred_element_type=jnp.float32,
    )
    partial_value = lax.psum_scatter(
        projected.astype(jnp.bfloat16), "mp", scatter_dimension=1, tiled=True
    ).astype(jnp.float32)
    stream_share = (
        lax.dynamic_slice_in_dim(stream, offset, quarter, 1) + share(mods[2]) * partial_value
    )
    stream = lax.all_gather(stream_share.astype(jnp.bfloat16), "mp", axis=1, tiled=True).astype(
        stream_share.dtype
    )
    normed = layer_norm(stream, mods[3], mods[4]).astype(jnp.bfloat16)
    upward = row_product(normed, lax.all_gather(w_in, "seq", axis=1, tiled=True)[0])
    hidden = jax.nn.gelu(upward, approximate=True).astype(jnp.bfloat16)
    downward = jnp.dot(
        hidden,
        lax.all_gather(w_out, "seq", axis=2, tiled=True)[0],
        preferred_element_type=jnp.float32,
    )
    mlp_part = lax.psum_scatter(
        downward.astype(jnp.bfloat16), "mp", scatter_dimension=1, tiled=True
    ).astype(jnp.float32)
    section_out = stream_share + share(mods[5]) * mlp_part
    moved = lax.all_to_all(
        lax.all_to_all(
            section_out[None, None].astype(jnp.bfloat16),
            "seq",
            split_axis=2,
            concat_axis=1,
            tiled=True,
        ),
        "branch",
        split_axis=2,
        concat_axis=0,
        tiled=True,
    ).astype(jnp.float32)
    frames = moved.shape[1]
    positions = moved.shape[2]
    rows = frames * positions
    control = moved[0]
    main_share = moved[1].reshape(rows, quarter)
    picks = (inject_layer[:, None] == jnp.arange(HINT_LAYERS, dtype=jnp.int32)[None, :]).astype(
        jnp.float32
    )
    gain = jnp.sum(picks[:, :, None] * hint_gain[None, :, :], axis=1)
    control_whole = lax.all_gather(control.astype(jnp.bfloat16), "mp", axis=2, tiled=True).astype(
        control.dtype
    )
    hint_in = (control_whole * gain[:, None, :]).astype(jnp.bfloat16).reshape(rows, D)
    hint = row_product(hint_in, lax.all_gather(hint_weight, "seq", axis=0, tiled=True))
    joined_share = main_share + hint
    joined = lax.all_gather(joined_share.astype(jnp.bfloat16), "mp", axis=1, tiled=True).astype(
        joined_share.dtype
    )
    normed_t = layer_norm(joined, t_mod[0], t_mod[1]).astype(jnp.bfloat16)
    piece = lax.all_gather(t_qkv, "seq", axis=0, tiled=True)
    tqkv = row_product(normed_t, piece.reshape(piece.shape[0], 3 * quarter))
    tqkv = tqkv.reshape(frames, positions, 3, local_heads, HEAD_DIM).transpose(1, 0, 2, 3, 4)
    attended_t = jax.vmap(attend)(tqkv[:, :, 0], tqkv[:, :, 1], tqkv[:, :, 2])
    attended_t = attended_t.transpose(1, 0, 2).reshape(rows, quarter).astype(jnp.bfloat16)
    projected_t = jnp.dot(
        attended_t,
        lax.all_gather(t_out, "seq", axis=1, tiled=True),
        preferred_element_type=jnp.float32,
    )
    temporal_part = lax.psum_scatter(
        projected_t.astype(jnp.bfloat16), "mp", scatter_dimension=1, tiled=True
    ).astype(jnp.float32)
    result = joined_share + share(t_mod[2]) * temporal_part
    return result.reshape(frames, positions, quarter)

F32, BF16 = jnp.float32, jnp.bfloat16


def dot(left, right):
    return jnp.dot(left, right, preferred_element_type=F32)


def dot_nt(left, right):
    return lax.dot_general(left, right, (((1,), (1,)), ((), ())), preferred_element_type=F32)


def fused_kernel(ring, *refs):
    n_weights = 6
    x_ref, mod_ref, gain_ref, tmod_ref = refs[:4]
    shards = refs[4 : 4 + n_weights]
    out_ref = refs[4 + n_weights]
    scratch = refs[5 + n_weights :]
    bufs = scratch[:n_weights]
    (qkv_ref, att_ref, x1_ref, send_ref, got_ref, got2_ref, hid_ref, yb_ref, moved_ref,
     js_ref, jr_ref, ts_ref, tr_ref, tq_ref, ta_ref, jf_ref) = scratch[n_weights : n_weights + 16]
    local_sem, right_sem, left_sem, z_sem, ysend_sem, y_sem, pair_send, pair_recv, move_send, move_recv, core_send, core_recv = (
        scratch[n_weights + 16 :]
    )
    group, seq, mp, branch = (lax.axis_index(a) for a in ("groups", "seq", "mp", "branch"))
    depth = shards[0].shape[0]
    half = depth // 2
    other = 1 - group
    quarter = js_ref.shape[1]
    heads = quarter // HEAD_DIM

    def at(z=None, g=None, m=None, b=None):
        return (
            group if g is None else g,
            seq if z is None else z,
            mp if m is None else m,
            branch if b is None else b,
        )

    def remote(src, dst, send, recv, device):
        return pltpu.make_async_remote_copy(
            src_ref=src, dst_ref=dst, send_sem=send, recv_sem=recv,
            device_id=device, device_id_type=pl.DeviceIdType.MESH,
        )

    shared = 4
    locals_ = []
    for w in range(n_weights):
        copy = pltpu.make_async_copy(
            shards[w],
            bufs[w].at[:, pl.ds(seq * depth, depth)] if w == shared else bufs[w].at[pl.ds(seq * depth, depth)],
            local_sem.at[w],
        )
        copy.start()
        locals_.append(copy)

    partners = [
        (lax.rem(seq + dz, ring), lax.rem(branch + db, 2))
        for dz in range(ring)
        for db in range(2)
        if dz or db
    ]
    barrier = pltpu.get_barrier_semaphore()
    greeted = [at(z=z, b=b) for z, b in partners] + [at(g=other), at(m=1 - mp)]
    for device in greeted:
        pl.semaphore_signal(barrier, inc=1, device_id=device, device_id_type=pl.DeviceIdType.MESH)
    pl.semaphore_wait(barrier, len(greeted))

    def block(w, s, g):
        rows = pl.ds(s * depth + g * half, half)
        return bufs[w].at[branch, rows] if w == shared else bufs[w].at[rows]

    def over(kind, s):
        ref = block(shared, s, other if kind else group)
        return remote(ref, ref, core_send.at[kind, s], core_recv.at[kind, s], at(b=1 - branch))

    def over_wait(kind, s):
        g = other if kind else group
        ref = bufs[shared].at[1 - branch, pl.ds(s * depth + g * half, half)]
        remote(ref, ref, core_send.at[kind, s], core_recv.at[kind, s], at(b=1 - branch)).wait_recv()

    def rightward(w, s):
        ref = block(w, s, group)
        return remote(ref, ref, right_sem.at[w, s], z_sem.at[w, s], at(z=lax.rem(seq + 1, ring)))

    def leftward(w, s):
        ref = block(w, s, group)
        return remote(ref, ref, left_sem.at[w, s], z_sem.at[w, s], at(z=lax.rem(seq + ring - 1, ring)))

    def across(w, s, g):
        ref = block(w, s, g)
        return remote(ref, ref, ysend_sem.at[w, s], y_sem.at[w, s], at(g=other))

    def own(w):
        locals_[w].wait()

        @pl.when(seq < ring - 1)
        def _():
            rightward(w, seq).start()

        @pl.when(seq > 0)
        def _():
            leftward(w, seq).start()

    def step(w, d):
        @pl.when(seq - d >= 0)
        def _():
            s = seq - d
            rightward(w, s).wait_recv()

            @pl.when(seq < ring - 1)
            def _():
                rightward(w, s).start()

            across(w, s, group).start()
            if w == shared:
                over(0, s).start()

        @pl.when(seq + d < ring)
        def _():
            s = seq + d
            leftward(w, s).wait_recv()

            @pl.when(seq > 0)
            def _():
                leftward(w, s).start()

            across(w, s, group).start()
            if w == shared:
                over(0, s).start()

    def finish(w):
        for d in range(1, ring):

            for sign in (-1, 1):
                s = seq + sign * d

                @pl.when((s >= 0) & (s < ring))
                def _():
                    across(w, s, other).wait_recv()
                    if w == shared:
                        over(1, s).start()

    def finish_shared():
        for d in range(1, ring):
            for sign in (-1, 1):
                s = seq + sign * d

                @pl.when((s >= 0) & (s < ring))
                def _():
                    over_wait(0, s)
                    over_wait(1, s)

    def drain(w):
        @pl.when(seq < ring - 1)
        def _():
            rightward(w, seq).wait_send()

        @pl.when(seq > 0)
        def _():
            leftward(w, seq).wait_send()

        for d in range(1, ring):

            @pl.when(seq - d >= 0)
            def _():
                across(w, seq - d, group).wait_send()
                if w == shared:
                    over(0, seq - d).wait_send()
                    over(1, seq - d).wait_send()

                @pl.when(seq < ring - 1)
                def _():
                    rightward(w, seq - d).wait_send()

            @pl.when(seq + d < ring)
            def _():
                across(w, seq + d, group).wait_send()
                if w == shared:
                    over(0, seq + d).wait_send()
                    over(1, seq + d).wait_send()

                @pl.when(seq > 0)
                def _():
                    leftward(w, seq + d).wait_send()

    def pair(i, src, dst):
        return remote(src, dst, pair_send.at[i], pair_recv.at[i], at(m=1 - mp))

    scale = 1.0 / (HEAD_DIM**0.5)
    own(0)
    own(1)
    own(2)
    normed = layer_norm(x_ref[...], mod_ref[0:1], mod_ref[1:2]).astype(BF16)
    step(0, 1)
    own(3)
    for d in range(2, ring):
        step(0, d)
    step(1, 1)
    own(4)
    for d in range(2, ring):
        step(1, d)
    finish(0)
    qkv_ref[...] = dot(normed, bufs[0][...])
    for i in range(heads):
        lo = i * HEAD_DIM
        query = (qkv_ref[:, lo : lo + HEAD_DIM] * scale).astype(BF16)
        keys = qkv_ref[:, quarter + lo : quarter + lo + HEAD_DIM].astype(BF16)
        values = qkv_ref[:, 2 * quarter + lo : 2 * quarter + lo + HEAD_DIM].astype(BF16)
        weights = jnp.exp(dot_nt(query, keys))
        total = jnp.sum(weights, axis=-1, keepdims=True)
        att_ref[:, lo : lo + HEAD_DIM] = dot(weights.astype(BF16), values) / total
        if i == heads // 2:
            step(2, 1)
            own(5)
    finish(1)
    projected = dot_nt(att_ref[...].astype(BF16), bufs[1][...])
    send_ref[0] = projected.astype(BF16)
    pair0 = pair(0, send_ref.at[0], got_ref)
    pair0.start()
    x1_ref[...] = x_ref[...] + mod_ref[2:3] * projected
    step(2, 2) if ring > 2 else None
    pair0.wait_recv()
    x1_ref[...] += mod_ref[2:3] * got_ref[...].astype(F32)
    normed = layer_norm(x1_ref[...], mod_ref[3:4], mod_ref[4:5]).astype(BF16)
    for d in range(3, ring):
        step(2, d)
    step(3, 1)
    finish(2)
    send_ref[1] = normed
    wide = bufs[2].shape[1]
    tile = 768 if wide % 768 == 0 else wide

    def up(c, _):
        cols = pl.ds(pl.multiple_of(c * tile, tile), tile)
        hid_ref[:, cols] = jax.nn.gelu(dot(send_ref[1], bufs[2][:, cols]), approximate=True).astype(BF16)
        return 0

    lax.fori_loop(0, wide // tile, up, 0)
    for d in range(2, ring):
        step(3, d)
    step(4, 1)
    finish(3)
    down = dot_nt(hid_ref[...], bufs[3][...])
    send_ref[2] = down.astype(BF16)
    pair1 = pair(1, send_ref.at[2], got2_ref)
    pair1.start()
    x1_ref[...] += mod_ref[5:6] * down
    for d in range(2, ring):
        step(4, d)
    step(5, 1)
    pair1.wait_recv()
    yb_ref[...] = (x1_ref[...] + mod_ref[5:6] * got2_ref[...].astype(F32)).astype(BF16)
    positions = moved_ref.shape[2]

    def rows_of(z, b):
        return pl.ds(pl.multiple_of((z * 2 + b) * positions, positions), positions)

    sends = []
    for i, (z, b) in enumerate(partners):
        copy = remote(
            yb_ref.at[rows_of(z, b)], moved_ref.at[branch, seq],
            move_send.at[i], move_recv.at[branch, seq], at(z=z, b=b),
        )
        copy.start()
        sends.append(copy)
    moved_ref[branch, seq] = yb_ref[rows_of(seq, branch), :]
    for d in range(2, ring):
        step(5, d)
    finish(4)
    for z, b in partners:
        remote(
            yb_ref.at[rows_of(seq, branch)], moved_ref.at[b, z],
            move_send.at[0], move_recv.at[b, z], at(z=z, b=b),
        ).wait_recv()
    finish_shared()
    rows = ring * positions
    hint_in = (moved_ref[0].astype(F32) * gain_ref[...][:, None, :]).astype(BF16)
    hint = dot(hint_in.reshape(rows, D), bufs[4][1, :, quarter:])
    main = moved_ref[1].astype(F32).reshape(rows, D)
    first = mp == 0

    def share(value):
        return jnp.where(first, value[:, :quarter], value[:, quarter:])

    joined_share = share(main) + hint
    js_ref[...] = joined_share.astype(BF16)
    pair2 = pair(2, js_ref, jr_ref)
    pair2.start()
    pair2.wait_recv()
    mine, theirs = joined_share, jr_ref[...].astype(F32)
    jf_ref[:, :quarter] = jnp.where(first, mine, theirs)
    jf_ref[:, quarter:] = jnp.where(first, theirs, mine)
    normed = layer_norm(jf_ref[...], tmod_ref[0:1], tmod_ref[1:2]).astype(BF16)
    tq_ref[:, : 2 * quarter] = dot(normed, bufs[4][0])
    tq_ref[:, 2 * quarter :] = dot(normed, bufs[4][1, :, :quarter])
    place = lax.rem(lax.broadcasted_iota(jnp.int32, (rows, rows), 0), positions)
    place_k = lax.rem(lax.broadcasted_iota(jnp.int32, (rows, rows), 1), positions)
    same = place == place_k
    for i in range(heads):
        lo = i * HEAD_DIM
        query = (tq_ref[:, lo : lo + HEAD_DIM] * scale).astype(BF16)
        keys = tq_ref[:, quarter + lo : quarter + lo + HEAD_DIM].astype(BF16)
        values = tq_ref[:, 2 * quarter + lo : 2 * quarter + lo + HEAD_DIM].astype(BF16)
        weights = jnp.where(same, jnp.exp(dot_nt(query, keys)), 0.0)
        total = jnp.sum(weights, axis=-1, keepdims=True)
        ta_ref[:, lo : lo + HEAD_DIM] = dot(weights.astype(BF16), values) / total
    finish(5)
    projected = dot_nt(ta_ref[...].astype(BF16), bufs[5][...])
    ts_ref[...] = jnp.where(first, projected[:, quarter:], projected[:, :quarter]).astype(BF16)
    pair3 = pair(3, ts_ref, tr_ref)
    pair3.start()
    for w in range(n_weights):
        drain(w)
    for copy in sends:
        copy.wait_send()
    pair3.wait_recv()
    gate = share(tmod_ref[2:3])
    out_ref[...] = joined_share + gate * (share(projected) + tr_ref[...].astype(F32))
    for copy in (pair0, pair1, pair2, pair3):
        copy.wait_send()


def fused(
    streams, modulation, s_qkv, s_out, w_in, w_out, hint_gain, inject_layer, hint_weight, t_mod, t_qkv, t_out
):
    ring = inject_layer.shape[0]
    tokens, quarter = streams.shape[2], s_qkv.shape[3]
    positions = tokens // (2 * ring)
    rows = ring * positions
    gain = hint_gain[inject_layer]
    depth = s_qkv.shape[1]
    shards = [
        s_qkv[0].reshape(depth, 3 * quarter),
        s_out[0].T,
        w_in[0],
        w_out[0].T,
        jnp.concatenate([t_qkv.reshape(depth, 3 * quarter), hint_weight], axis=1)
        .reshape(depth, 2, 2 * quarter)
        .transpose(1, 0, 2),
        t_out.T,
    ]
    n = len(shards)
    dma = pltpu.SemaphoreType.DMA
    vmem = pl.BlockSpec(memory_space=pltpu.VMEM)
    anywhere = pl.BlockSpec(memory_space=pl.ANY)
    out = pl.pallas_call(
        functools.partial(fused_kernel, ring),
        out_shape=jax.ShapeDtypeStruct((rows, quarter), F32),
        in_specs=[vmem] * 4 + [anywhere] * n,
        out_specs=vmem,
        scratch_shapes=[pltpu.VMEM(a.shape[:-2] + (ring * depth, a.shape[-1]), BF16) for a in shards]
        + [
            pltpu.VMEM((tokens, 3 * quarter), F32),
            pltpu.VMEM((tokens, quarter), F32),
            pltpu.VMEM((tokens, D), F32),
            pltpu.VMEM((3, tokens, D), BF16),
            pltpu.VMEM((tokens, D), BF16),
            pltpu.VMEM((tokens, D), BF16),
            pltpu.VMEM((tokens, w_in.shape[2]), BF16),
            pltpu.VMEM((tokens, D), BF16),
            pltpu.VMEM((2, ring, positions, D), BF16),
            pltpu.VMEM((rows, quarter), BF16),
            pltpu.VMEM((rows, quarter), BF16),
            pltpu.VMEM((rows, quarter), BF16),
            pltpu.VMEM((rows, quarter), BF16),
            pltpu.VMEM((rows, 3 * quarter), F32),
            pltpu.VMEM((rows, quarter), F32),
            pltpu.VMEM((rows, D), F32),
            dma((n,)),
            dma((n, ring)),
            dma((n, ring)),
            dma((n, ring)),
            dma((n, ring)),
            dma((n, ring)),
            dma((4,)),
            dma((4,)),
            dma((2 * ring - 1,)),
            dma((2, ring)),
            dma((2, ring)),
            dma((2, ring)),
        ],
        compiler_params=pltpu.CompilerParams(
            collective_id=0, has_side_effects=True, vmem_limit_bytes=50 * 1024 * 1024
        ),
    )(streams[0, 0], modulation[0], gain, t_mod, *shards)
    return out.reshape(ring, positions, quarter)


def solution(mesh):
    sizes = dict(mesh.shape)
    fits = (sizes["groups"], sizes["mp"], sizes["branch"]) == (2, 2, 2) and sizes["seq"] in (2, 4)
    in_specs = (
        P("branch", ("groups", "seq"), None, None),
        P("branch", None, None),
        P("branch", "seq", None, "mp"),
        P("branch", "mp", "seq"),
        P("branch", "seq", "mp"),
        P("branch", "mp", "seq"),
        P(),
        P(),
        P("seq", "mp"),
        P(),
        P("seq", None, "mp"),
        P("mp", "seq"),
    )
    out_specs = P("groups", ("seq", "branch"), "mp")
    return jax.shard_map(
        fused if fits else on_device, mesh=mesh, in_specs=in_specs, out_specs=out_specs, check_vma=False
    )
```
